32 devices in a mesh: dp: 4 (over x, core), mem: 8 (over z, y).
Axes of the slice: x: 2, y: 2, z: 4, core: 2. Of those that a mesh axis runs over, the one named last changes fastest.
Arguments:
- tokens: bfloat16 [16384, 2048], P(('dp', 'mem')), may hold values from -6 to 6
- span_bounds: int32 [2, 1024], P(None, ('dp', 'mem')), may hold values from 0 to 512, as said below
- mention_entity: int32 [1024], P(('dp', 'mem')), may hold values from 0 to 1023, as said below
- entity_cluster: int32 [1024], P('mem'), may hold values from 0 to 63, as said below
- entity_table: bfloat16 [1024, 2048], P('mem'), may hold values from -16 to 16
- w_out: bfloat16 [2048, 2048], replicated, may hold values from -0.125 to 0.125
Outputs:
- memory_out: bfloat16 [16384, 2048], P(('dp', 'mem'))
The draws below stay inside these ranges and needn't reach their ends.
Inputs may be any that keep to these rules, and one draw needn't show every extreme that they name: `span_bounds`: mention i lies in segment i // 32; row 0 holds its start and row 1 its exclusive end, counted from the segment's first token, with start < end. `mention_entity`: entity e belongs to memory shard e // 128. Among the 32 mentions of each device, those naming entities of one shard number exactly 4, and those of every other shard number (28) // 7 or one more. `entity_cluster`: each cluster holds exactly 16 entities.
All inputs are finite; a program needn't handle non-finite values.
Results may differ from the reference program's by a relative error of at most 0.017.
Values may be sent and summed in bfloat16 or wider, within the bound.
A program may use at most 320 MiB of HBM per device.

```python
import jax
import jax.numpy as jnp
from jax import lax

D = 2048
HEADS = 32
HEAD_DIM = 64
SEG = 512
MENT_SEG = 32
ENT_DEV = 128
MENT_DEV = 32
CAP = 4
ENTITIES = 1024
CLUSTERS = 64
TOKENS = 16384
MENTIONS = 1024
N_MEM = 8


def cluster_ids(key):
    cluster_key = jax.random.fold_in(key, 13)
    shuffled = jax.random.permutation(cluster_key, ENTITIES)
    return (shuffled % CLUSTERS).astype(jnp.int32)


def draw_tokens(key, part):
    key = jax.random.fold_in(key, 21)
    base_key = jax.random.fold_in(key, 0)
    values = jnp.clip(jax.random.normal(base_key, (TOKENS, D)), -6.0, 6.0)
    return values.astype(jnp.bfloat16)


def draw_entity_table(key, part):
    key = jax.random.fold_in(key, 22)
    base_key = jax.random.fold_in(key, 0)
    values = jnp.clip(jax.random.normal(base_key, (ENTITIES, D)), -6.0, 6.0)
    return values.astype(jnp.bfloat16)


def draw_span_bounds(key, part):
    key = jax.random.fold_in(key, 12)
    first_key, second_key = jax.random.split(key)
    longest = max(1, min(16, SEG // 2))
    span_len = jax.random.randint(first_key, (MENTIONS,), 1, longest + 1)
    starts = jax.random.randint(second_key, (MENTIONS,), 0, SEG - span_len + 1)
    in_segment = jnp.arange(MENTIONS, dtype=jnp.int32) % MENT_SEG
    starts = jnp.where(in_segment == 0, SEG - span_len, jnp.where(in_segment == 1, 0, starts))
    return jnp.stack([starts, starts + span_len]).astype(jnp.int32)


def draw_mention_entity(key, part):
    key = jax.random.fold_in(key, 11)
    hot_key, inner_key, order_key = jax.random.split(key, 3)
    blocks = MENTIONS // MENT_DEV
    hot_shard = jax.random.randint(hot_key, (blocks, 1), 0, N_MEM)
    row_index = jnp.arange(MENT_DEV, dtype=jnp.int32)[None, :]
    spread = (hot_shard + 1 + (row_index - CAP) % (N_MEM - 1)) % N_MEM
    owner_shard = jnp.where(row_index < CAP, hot_shard, spread)
    inside = jax.random.randint(inner_key, (blocks, MENT_DEV), 0, ENT_DEV)
    last_shard = owner_shard == N_MEM - 1
    first_last = last_shard & (jnp.cumsum(last_shard.astype(jnp.int32), axis=1) == 1)
    zero_shard = owner_shard == 0
    first_zero = zero_shard & (jnp.cumsum(zero_shard.astype(jnp.int32), axis=1) == 1)
    inside = jnp.where(first_last, ENT_DEV - 1, jnp.where(first_zero, 0, inside))
    entity_ids = owner_shard * ENT_DEV + inside
    order_scores = jax.random.randint(order_key, (blocks, MENT_DEV), 0, 1 << 20) * MENT_DEV + row_index
    ordering = jnp.argsort(order_scores, axis=1)
    return jnp.take_along_axis(entity_ids, ordering, axis=1).reshape(-1).astype(jnp.int32)


def draw_entity_cluster(key, part):
    return cluster_ids(key)


def scatter_about(rng, dims, width, most, kind=jnp.bfloat16):
    result = jax.random.normal(rng, dims, jnp.float32) * width
    return jnp.minimum(jnp.maximum(result, -most), most).astype(kind)


def setup_inputs(seed: int = 0) -> dict:
    key_list = jax.random.split(jax.random.key(seed), 7)
    return {
        "tokens": draw_tokens(jax.random.fold_in(key_list[6], 71), 0),
        "span_bounds": draw_span_bounds(jax.random.fold_in(key_list[6], 71), 0),
        "mention_entity": draw_mention_entity(jax.random.fold_in(key_list[6], 71), 0),
        "entity_cluster": draw_entity_cluster(jax.random.fold_in(key_list[6], 71), 0),
        "entity_table": draw_entity_table(jax.random.fold_in(key_list[6], 71), 0),
        "w_out": scatter_about(key_list[5], (D, D), D ** -0.5, 0.125),
    }


def rms_rows(values):
    return values * lax.rsqrt(lax.optimization_barrier(jnp.mean(values * values, axis=-1, keepdims=True)) + 1e-06)

def mention_vectors(tokens, span_bounds):
    segments = tokens.shape[0] // SEG
    seg_tokens = tokens.reshape(segments, SEG, D).astype(jnp.float32)
    starts = span_bounds[0].reshape(segments, MENT_SEG)
    ends = span_bounds[1].reshape(segments, MENT_SEG)
    positions = jnp.arange(SEG, dtype=jnp.int32)
    covered = ((positions[None, None, :] >= starts[:, :, None]) & (positions[None, None, :] < ends[:, :, None])).astype(jnp.float32)
    span_sums = jnp.einsum('smp,spd->smd', covered, seg_tokens)
    span_len = (ends - starts).astype(jnp.float32)
    return (span_sums / span_len[:, :, None]).reshape(segments * MENT_SEG, D).astype(jnp.bfloat16)

def attend(queries, memory):
    scale = HEAD_DIM ** (-0.5)
    scores = jnp.einsum('thd,khd->htk', queries.astype(jnp.float32), memory.astype(jnp.float32)) * scale
    probs = jnp.exp(scores - lax.optimization_barrier(jnp.max(scores, axis=-1, keepdims=True)))
    totals = lax.optimization_barrier(jnp.sum(probs, axis=-1))
    rounded = lax.optimization_barrier(probs.astype(jnp.bfloat16))
    weighted = jnp.einsum('htk,khd->thd', rounded.astype(jnp.float32), memory.astype(jnp.float32))
    return weighted / jnp.transpose(totals)[:, :, None]

def reference(tokens, span_bounds, mention_entity, entity_cluster, entity_table, w_out):
    mention_vec = mention_vectors(tokens, span_bounds)
    pooled = jax.ops.segment_sum(mention_vec.astype(jnp.float32), mention_entity, num_segments=ENTITIES)
    entity_state = rms_rows(entity_table.astype(jnp.float32) + pooled).astype(jnp.bfloat16)
    grouped = jax.ops.segment_sum(entity_state.astype(jnp.float32), entity_cluster, num_segments=CLUSTERS)
    cluster_state = rms_rows(grouped).astype(jnp.bfloat16)
    entity_heads = entity_state.reshape(ENTITIES, HEADS, HEAD_DIM)
    cluster_heads = cluster_state.reshape(CLUSTERS, HEADS, HEAD_DIM)

    def one_segment(segment):
        queries = segment.reshape(SEG, HEADS, HEAD_DIM)
        readout = (attend(queries, entity_heads) + attend(queries, cluster_heads)).astype(jnp.bfloat16).reshape(SEG, D)
        projected = jnp.dot(readout, w_out, preferred_element_type=jnp.float32)
        return rms_rows(projected).astype(jnp.bfloat16)
    memory_out = lax.map(one_segment, tokens.reshape(-1, SEG, D))
    return memory_out.reshape(-1, D)
```

```python
import functools

import jax
import jax.numpy as jnp
from jax import lax
from jax.experimental import pallas as pl
from jax.experimental.pallas import tpu as pltpu
from jax.sharding import PartitionSpec as P

MESH = pl.DeviceIdType.MESH
HEAD_DIM = 64
CL_SIZE = 16
SLOTS = 4
PIECES = 4
BF16 = jnp.bfloat16
F32 = jnp.float32


def rms_rows(values):
    return values * lax.rsqrt(jnp.mean(values * values, axis=-1, keepdims=True) + 1e-06)


def ring_place(index, depth, width):
    z, y = index // width, index % width
    back = depth - 1 - z
    across = jnp.where(back % 2 == 0, y - 1, width - 1 - y)
    return jnp.where(y == 0, z, depth + back * (width - 1) + across)


def ring_device(place, depth, width):
    rest = jnp.maximum(place - depth, 0)
    back, across = rest // (width - 1), rest % (width - 1)
    y = jnp.where(back % 2 == 0, 1 + across, width - 1 - across)
    return jnp.where(place < depth, place * width, (depth - 1 - back) * width + y)


def exchange_kernel(
    n, groups, tokens, bounds, ent_col, ent_row, cluster_col, table,
    states_out, cluster_out,
    outbox, mentions, states, pooled,
    mem_send, mem_recv, dp_send, dp_recv, pair_send, pair_recv, own_sem,
    ring_send, ring_recv, hand_send, hand_recv, out_sem,
):
    d = table.shape[1]
    rows = table.shape[0]
    piece = d // PIECES
    depth, width = 4, n // 4
    me, row = lax.axis_index("mem"), lax.axis_index("dp")
    core = row % 2
    sibling = row + 1 - 2 * core
    place = ring_place(me, depth, width)
    right = ring_device((place + 1) % n, depth, width)
    left = ring_device((place + n - 1) % n, depth, width)
    xs = groups // 2

    barrier = pltpu.get_barrier_semaphore()
    for step in range(1, n):
        pl.semaphore_signal(barrier, device_id=(row, (me + step) % n), device_id_type=MESH)
    for step in range(1, xs):
        pl.semaphore_signal(barrier, device_id=((row + 2 * step) % groups, me), device_id_type=MESH)
    pl.semaphore_signal(barrier, device_id=(sibling, me), device_id_type=MESH)

    count = bounds.shape[0]
    position = lax.broadcasted_iota(jnp.int32, (count, tokens.shape[0]), 1)
    covered = (position >= bounds[:, 0:1]) & (position < bounds[:, 1:2])
    sums = jnp.dot(covered.astype(F32).astype(BF16), tokens[...], preferred_element_type=F32)
    vectors = (sums / (bounds[:, 1:2] - bounds[:, 0:1]).astype(F32)).astype(BF16)
    shard_col, shard_row = ent_col[...] // rows, ent_row[...] // rows
    first = lax.broadcasted_iota(jnp.int32, (count, count), 0)
    second = lax.broadcasted_iota(jnp.int32, (count, count), 1)
    rank = jnp.sum(((shard_col == shard_row) & (first < second)).astype(jnp.int32), axis=0, keepdims=True)
    slot_row = shard_row * SLOTS + rank
    total = n * SLOTS * PIECES
    line = lax.broadcasted_iota(jnp.int32, (total, count), 0)
    match = slot_row == (line // (SLOTS * PIECES)) * SLOTS + line % SLOTS
    part = (line // SLOTS) % PIECES
    packed = jnp.zeros((total, piece), F32)
    for p in range(PIECES):
        pick = (match & (part == p)).astype(F32).astype(BF16)
        packed += jnp.dot(pick, vectors[:, p * piece:(p + 1) * piece], preferred_element_type=F32)
    local = (ent_row[...] - shard_row * rows + 1).astype(F32)
    ids = jnp.sum(jnp.where(match, local, 0.0), axis=1, keepdims=True) - 1.0
    outbox[:, :, :piece] = packed.astype(BF16).reshape(n, SLOTS * PIECES, piece)
    outbox[:, :, piece:] = jnp.broadcast_to(ids, (total, 128)).astype(BF16).reshape(n, SLOTS * PIECES, 128)

    pl.semaphore_wait(barrier, n - 1 + xs)

    own = pltpu.make_async_copy(outbox.at[me], mentions.at[row, me], own_sem)
    own.start()
    sends = []
    for step in range(1, n):
        to = (me + step) % n
        copy = pltpu.make_async_remote_copy(
            outbox.at[to], mentions.at[row, me], mem_send.at[step], mem_recv.at[step],
            device_id=(row, to), device_id_type=MESH)
        copy.start()
        sends.append(copy)
    own.wait()
    for step in range(1, n):
        src = (me + n - step) % n
        pltpu.make_async_remote_copy(
            outbox.at[src], mentions.at[row, src], mem_send.at[step], mem_recv.at[step],
            device_id=(row, src), device_id_type=MESH).wait_recv()

    def to_replica(block, to, send, recv):
        return pltpu.make_async_remote_copy(
            mentions.at[block], mentions.at[block], send, recv, device_id=(to, me), device_id_type=MESH)

    for step in range(1, xs):
        copy = to_replica(row, (row + 2 * step) % groups, dp_send.at[step], dp_recv.at[step])
        copy.start()
        sends.append(copy)
    copy = to_replica(row, sibling, pair_send.at[0], pair_recv.at[0])
    copy.start()
    sends.append(copy)
    for step in range(1, xs):
        src = (row + groups - 2 * step) % groups
        to_replica(src, src, dp_send.at[step], dp_recv.at[step]).wait_recv()
        copy = to_replica(src, sibling, pair_send.at[step], pair_recv.at[step])
        copy.start()
        sends.append(copy)
    for step in range(xs):
        src = (sibling + groups - 2 * step) % groups
        to_replica(src, sibling, pair_send.at[step], pair_recv.at[step]).wait_recv()

    arrived = groups * n * SLOTS * PIECES
    box = mentions[...].reshape(arrived, piece + 128)
    line = lax.broadcasted_iota(jnp.int32, (arrived, rows), 0)
    entity = lax.broadcasted_iota(jnp.int32, (arrived, rows), 1).astype(F32)
    named = box[:, piece:].astype(F32) == entity
    part = (line // SLOTS) % PIECES
    square = jnp.zeros((rows, 1), F32)
    for p in range(PIECES):
        pick = (named & (part == p)).astype(F32).astype(BF16)
        got = lax.dot_general(pick, box[:, :piece], (((0,), (0,)), ((), ())), preferred_element_type=F32)
        got += table[:, p * piece:(p + 1) * piece].astype(F32)
        pooled[:, p * piece:(p + 1) * piece] = got
        square += jnp.sum(got * got, axis=-1, keepdims=True)
    state = (pooled[...] * lax.rsqrt(square / d + 1e-06)).astype(BF16)
    quarter = rows // 4
    states[0, :, :, :d] = state.reshape(4, quarter, d)
    kind = lax.broadcasted_iota(jnp.int32, (rows, 128), 1)
    group = (cluster_col[...] == kind).astype(F32).astype(BF16)
    states[0, :, :, d:] = group.reshape(4, quarter, 128)

    half = n // 2

    def portion(way, step):
        if step < half:
            return pl.ds(2 * core, 2)
        return pl.ds(2 * core + way, 1)

    def ring_copy(way, step):
        src = step - 1 if way == 0 else (n - step + 1) % n
        dst = step if way == 0 else n - step
        quarters = portion(way, step)
        return pltpu.make_async_remote_copy(
            states.at[src, quarters], states.at[dst, quarters], ring_send.at[way, step], ring_recv.at[way, step],
            device_id=(row, right if way == 0 else left), device_id_type=MESH)

    def hand_copy(way, step, to_core):
        dst = step if way == 0 else n - step
        if step < half:
            quarters = pl.ds(2 * to_core, 2)
        else:
            quarters = pl.ds(2 * to_core + way, 1)
        return pltpu.make_async_remote_copy(
            states.at[dst, quarters], states.at[dst, quarters], hand_send.at[way, step], hand_recv.at[way, step],
            device_id=(sibling, me), device_id_type=MESH)

    def out_copy(slot):
        return pltpu.make_async_copy(
            states.at[slot, :, :, pl.ds(0, d)], states_out.at[slot], out_sem.at[slot])

    outs = [out_copy(0)]
    outs[0].start()
    for step in range(1, half + 1):
        for way in range(2):
            if step > 1:
                ring_copy(way, step - 1).wait_recv()
            copy = ring_copy(way, step)
            copy.start()
            sends.append(copy)
            if step > 1:
                copy = hand_copy(way, step - 1, core)
                copy.start()
                sends.append(copy)
    for way in range(2):
        ring_copy(way, half).wait_recv()
        copy = hand_copy(way, half, core)
        copy.start()
        sends.append(copy)
    for step in range(1, half + 1):
        for way in range(2):
            hand_copy(way, step, 1 - core).wait_recv()
            if step < half:
                slot = step if way == 0 else n - step
                outs.append(out_copy(slot))
                outs[-1].start()
    outs.append(out_copy(half))
    outs[-1].start()

    clusters = cluster_out.shape[0]
    every = states[...].reshape(n * rows, d + 128)
    grouped = lax.dot_general(every[:, d:], every[:, :d], (((0,), (0,)), ((), ())), preferred_element_type=F32)
    cluster_out[...] = rms_rows(grouped[:clusters]).astype(BF16)
    for copy in outs:
        copy.wait()
    for copy in sends:
        copy.wait_send()


def exchange(n, groups, tokens, span_bounds, mention_entity, entity_cluster, table):
    rows, d = table.shape
    count = mention_entity.shape[0]
    clusters = rows * n // CL_SIZE
    piece = d // PIECES
    vmem = pl.BlockSpec(memory_space=pltpu.VMEM)
    dma = pltpu.SemaphoreType.DMA
    return pl.pallas_call(
        functools.partial(exchange_kernel, n, groups),
        out_shape=(jax.ShapeDtypeStruct((n, 4, rows // 4, d), BF16), jax.ShapeDtypeStruct((clusters, d), BF16)),
        in_specs=[vmem] * 6,
        out_specs=(pl.BlockSpec(memory_space=pl.ANY), vmem),
        scratch_shapes=[
            pltpu.VMEM((n, SLOTS * PIECES, piece + 128), BF16),
            pltpu.VMEM((groups, n, SLOTS * PIECES, piece + 128), BF16),
            pltpu.VMEM((n, 4, rows // 4, d + 128), BF16),
            pltpu.VMEM((rows, d), F32),
            dma((n,)), dma((n,)), dma((groups,)), dma((groups,)), dma((groups,)), dma((groups,)), dma,
            dma((2, n)), dma((2, n)), dma((2, n)), dma((2, n)), dma((n,)),
        ],
        compiler_params=pltpu.CompilerParams(
            collective_id=0, has_side_effects=True, vmem_limit_bytes=48 * 2**20),
    )(tokens, span_bounds.T, mention_entity.reshape(count, 1), mention_entity.reshape(1, count),
      entity_cluster.reshape(rows, 1), table)


def read_kernel(q_ref, k_ref, c_ref, w_hbm, out_ref, readout, weights, sem):
    g = pl.program_id(0)
    width = q_ref.shape[1]
    load = pltpu.make_async_copy(w_hbm, weights, sem)

    @pl.when(g == 0)
    def _():
        load.start()

    low = lax.broadcasted_iota(jnp.int32, (1, width), 1) < HEAD_DIM
    one, zero = jnp.ones((), BF16), jnp.zeros((), BF16)
    q = q_ref[...] * BF16(HEAD_DIM ** -0.5)
    queries = (jnp.where(low, q, zero), jnp.where(low, zero, q))
    total = None
    for ref in (k_ref, c_ref):
        keys = ref[...]
        values = (jnp.where(low, keys, one), jnp.where(low, one, keys))
        sides = []
        for h in range(2):
            scores = lax.dot_general(
                queries[h], keys, (((1,), (1,)), ((), ())), preferred_element_type=F32)
            probs = jnp.exp(scores - jnp.max(scores, axis=-1, keepdims=True)).astype(BF16)
            sides.append(jnp.dot(probs, values[h], preferred_element_type=F32))
        read = jnp.where(low, sides[0], sides[1]) / pltpu.roll(
            jnp.where(low, sides[1], sides[0]), HEAD_DIM, 1)
        total = read if total is None else total + read
    readout[:, pl.ds(pl.multiple_of(g * width, width), width)] = total.astype(BF16)

    @pl.when(g == pl.num_programs(0) - 1)
    def _():
        load.wait()
        projected = jnp.dot(readout[...], weights[...], preferred_element_type=F32)
        out_ref[...] = rms_rows(projected).astype(BF16)


def read_memories(queries, keys, clusters, w_out):
    tokens, d = queries.shape
    width = 2 * HEAD_DIM
    columns = lambda g: (0, g)
    return pl.pallas_call(
        read_kernel,
        grid=(d // width,),
        in_specs=[
            pl.BlockSpec((tokens, width), columns),
            pl.BlockSpec((keys.shape[0], width), columns),
            pl.BlockSpec((clusters.shape[0], width), columns),
            pl.BlockSpec(memory_space=pl.ANY),
        ],
        out_specs=pl.BlockSpec((tokens, d), lambda g: (0, 0)),
        out_shape=jax.ShapeDtypeStruct((tokens, d), BF16),
        scratch_shapes=[pltpu.VMEM((tokens, d), BF16), pltpu.VMEM(w_out.shape, BF16), pltpu.SemaphoreType.DMA],
        compiler_params=pltpu.CompilerParams(vmem_limit_bytes=48 * 2**20),
    )(queries, keys, clusters, w_out)


def on_device(tokens, span_bounds, mention_entity, entity_cluster, entity_table, w_out):
    n, groups = lax.axis_size("mem"), lax.axis_size("dp")
    states, clusters = exchange(
        n, groups, tokens, span_bounds, mention_entity, entity_cluster, entity_table)
    return read_memories(tokens, states.reshape(-1, tokens.shape[1]), clusters, w_out)


def solution(mesh):
    placed = (
        P(("dp", "mem"), None),
        P(None, ("dp", "mem")),
        P(("dp", "mem")),
        P("mem"),
        P("mem", None),
        P(),
    )
    return jax.shard_map(
        on_device, mesh=mesh, in_specs=placed, out_specs=P(("dp", "mem"), None), check_vma=False
    )
```

```python
import functools

import jax
import jax.numpy as jnp
from jax import lax
from jax.experimental import pallas as pl
from jax.experimental.pallas import tpu as pltpu
from jax.sharding import PartitionSpec as P

MESH = pl.DeviceIdType.MESH
HEAD_DIM = 64
CL_SIZE = 16
SLOTS = 4
PIECES = 4
BF16 = jnp.bfloat16
F32 = jnp.float32


def rms_rows(values):
    return values * lax.rsqrt(jnp.mean(values * values, axis=-1, keepdims=True) + 1e-06)


def ring_place(index, depth, width):
    z, y = index // width, index % width
    back = depth - 1 - z
    across = jnp.where(back % 2 == 0, y - 1, width - 1 - y)
    return jnp.where(y == 0, z, depth + back * (width - 1) + across)


def ring_device(place, depth, width):
    rest = jnp.maximum(place - depth, 0)
    back, across = rest // (width - 1), rest % (width - 1)
    y = jnp.where(back % 2 == 0, 1 + across, width - 1 - across)
    return jnp.where(place < depth, place * width, (depth - 1 - back) * width + y)


def fused_kernel(
    n, groups, bounds, ent_row, cluster_row, tokens_hbm, table_hbm, w_hbm,
    out_ref,
    tokens, table, weights, outbox, mentions, states, pooled, clusters, num, den, top, readout,
    load_sem, mem_send, mem_recv, dp_send, dp_recv, pair_send, pair_recv, own_sem,
    ring_send, ring_recv, hand_send, hand_recv,
):
    loads = [
        pltpu.make_async_copy(src, dst, load_sem.at[i])
        for i, (src, dst) in enumerate(((tokens_hbm, tokens), (table_hbm, table), (w_hbm, weights)))
    ]
    for load in loads:
        load.start()
    d = table.shape[1]
    rows = table.shape[0]
    piece = d // PIECES
    depth, width = 4, n // 4
    me, row = lax.axis_index("mem"), lax.axis_index("dp")
    core = row % 2
    sibling = row + 1 - 2 * core
    place = ring_place(me, depth, width)
    right = ring_device((place + 1) % n, depth, width)
    left = ring_device((place + n - 1) % n, depth, width)
    xs = groups // 2

    barrier = pltpu.get_barrier_semaphore()
    for step in range(1, n):
        pl.semaphore_signal(barrier, device_id=(row, (me + step) % n), device_id_type=MESH)
    for step in range(1, xs):
        pl.semaphore_signal(barrier, device_id=((row + 2 * step) % groups, me), device_id_type=MESH)
    pl.semaphore_signal(barrier, device_id=(sibling, me), device_id_type=MESH)

    count = bounds.shape[1]
    length = tokens.shape[0]
    total = n * SLOTS * PIECES
    position = lax.broadcasted_iota(jnp.int32, (length, count), 0)
    covered = ((position >= bounds[0:1, :]) & (position < bounds[1:2, :])).astype(F32).astype(BF16)
    spans = lax.dot_general(
        covered, jnp.ones((length, 128), BF16), (((0,), (0,)), ((), ())), preferred_element_type=F32)
    shard_row = ent_row[...] // rows
    owner = (lax.broadcasted_iota(jnp.int32, (n, count), 0) == shard_row).astype(F32)
    first = lax.broadcasted_iota(jnp.int32, (count, count), 0)
    second = lax.broadcasted_iota(jnp.int32, (count, count), 1)
    before = jnp.dot(
        owner.astype(BF16), (first < second).astype(F32).astype(BF16), preferred_element_type=F32)
    rank = jnp.sum(owner * before, axis=0, keepdims=True).astype(jnp.int32)
    slot_row = shard_row * SLOTS + rank
    loads[0].wait()
    sums = lax.dot_general(covered, tokens[...], (((0,), (0,)), ((), ())), preferred_element_type=F32)
    vectors = (sums / spans[:, 0:1]).astype(BF16)
    line = lax.broadcasted_iota(jnp.int32, (total, count), 0)
    match = slot_row == (line // (SLOTS * PIECES)) * SLOTS + line % SLOTS
    part = (line // SLOTS) % PIECES
    packed = jnp.zeros((total, piece), F32)
    for p in range(PIECES):
        pick = (match & (part == p)).astype(F32).astype(BF16)
        packed += jnp.dot(pick, vectors[:, p * piece:(p + 1) * piece], preferred_element_type=F32)
    local = (ent_row[...] - shard_row * rows + 1).astype(F32)
    ids = jnp.sum(jnp.where(match, local, 0.0), axis=1, keepdims=True) - 1.0
    outbox[:, :, :piece] = packed.astype(BF16).reshape(n, SLOTS * PIECES, piece)
    outbox[:, :, piece:] = jnp.broadcast_to(ids, (total, 128)).astype(BF16).reshape(n, SLOTS * PIECES, 128)

    pl.semaphore_wait(barrier, n - 1 + xs)

    own = pltpu.make_async_copy(outbox.at[me], mentions.at[row, me], own_sem)
    own.start()
    sends = []
    for step in range(1, n):
        to = (me + step) % n
        copy = pltpu.make_async_remote_copy(
            outbox.at[to], mentions.at[row, me], mem_send.at[step], mem_recv.at[step],
            device_id=(row, to), device_id_type=MESH)
        copy.start()
        sends.append(copy)
    own.wait()
    for step in range(1, n):
        src = (me + n - step) % n
        pltpu.make_async_remote_copy(
            outbox.at[src], mentions.at[row, src], mem_send.at[step], mem_recv.at[step],
            device_id=(row, src), device_id_type=MESH).wait_recv()

    def to_replica(block, to, send, recv):
        return pltpu.make_async_remote_copy(
            mentions.at[block], mentions.at[block], send, recv, device_id=(to, me), device_id_type=MESH)

    for step in range(1, xs):
        copy = to_replica(row, (row + 2 * step) % groups, dp_send.at[step], dp_recv.at[step])
        copy.start()
        sends.append(copy)
    copy = to_replica(row, sibling, pair_send.at[0], pair_recv.at[0])
    copy.start()
    sends.append(copy)
    for step in range(1, xs):
        src = (row + groups - 2 * step) % groups
        to_replica(src, src, dp_send.at[step], dp_recv.at[step]).wait_recv()
        copy = to_replica(src, sibling, pair_send.at[step], pair_recv.at[step])
        copy.start()
        sends.append(copy)
    for step in range(xs):
        src = (sibling + groups - 2 * step) % groups
        to_replica(src, sibling, pair_send.at[step], pair_recv.at[step]).wait_recv()

    loads[1].wait()
    arrived = groups * n * SLOTS * PIECES
    box = mentions[...].reshape(arrived, piece + 128)
    line = lax.broadcasted_iota(jnp.int32, (arrived, rows), 0)
    entity = lax.broadcasted_iota(jnp.int32, (arrived, rows), 1).astype(F32)
    named = box[:, piece:].astype(F32) == entity
    part = (line // SLOTS) % PIECES
    square = jnp.zeros((rows, 1), F32)
    for p in range(PIECES):
        pick = (named & (part == p)).astype(F32).astype(BF16)
        got = lax.dot_general(pick, box[:, :piece], (((0,), (0,)), ((), ())), preferred_element_type=F32)
        got += table[:, p * piece:(p + 1) * piece].astype(F32)
        pooled[:, p * piece:(p + 1) * piece] = got
        square += jnp.sum(got * got, axis=-1, keepdims=True)
    state = (pooled[...] * lax.rsqrt(square / d + 1e-06)).astype(BF16)
    quarter = rows // 4
    states[0, :, :, :d] = state.reshape(4, quarter, d)
    kind = lax.broadcasted_iota(jnp.int32, (128, rows), 0)
    group = (cluster_row[...] == kind).astype(F32).T.astype(BF16)
    states[0, :, :, d:] = group.reshape(4, quarter, 128)

    half = n // 2

    def portion(way, step):
        if step < half:
            return pl.ds(2 * core, 2)
        return pl.ds(2 * core + way, 1)

    def ring_copy(way, step):
        src = step - 1 if way == 0 else (n - step + 1) % n
        dst = step if way == 0 else n - step
        quarters = portion(way, step)
        return pltpu.make_async_remote_copy(
            states.at[src, quarters], states.at[dst, quarters], ring_send.at[way, step], ring_recv.at[way, step],
            device_id=(row, right if way == 0 else left), device_id_type=MESH)

    def hand_copy(way, step, to_core):
        dst = step if way == 0 else n - step
        if step < half:
            quarters = pl.ds(2 * to_core, 2)
        else:
            quarters = pl.ds(2 * to_core + way, 1)
        return pltpu.make_async_remote_copy(
            states.at[dst, quarters], states.at[dst, quarters], hand_send.at[way, step], hand_recv.at[way, step],
            device_id=(sibling, me), device_id_type=MESH)

    def serve(step):
        for way in range(2):
            ring_copy(way, step).wait_recv()
            if step < half:
                copy = ring_copy(way, step + 1)
                copy.start()
                sends.append(copy)
            copy = hand_copy(way, step, core)
            copy.start()
            sends.append(copy)

    for way in range(2):
        copy = ring_copy(way, 1)
        copy.start()
        sends.append(copy)

    width = 2 * HEAD_DIM
    low = lax.broadcasted_iota(jnp.int32, (1, width), 1) < HEAD_DIM
    one, zero = jnp.ones((), BF16), jnp.zeros((), BF16)

    def lanes_of(index, size):
        return pl.ds(pl.multiple_of(index * size, size), size)

    def read_part(lanes, slots):
        q = tokens[:, lanes] * BF16(HEAD_DIM ** -0.5)
        keys = jnp.concatenate([states[slot, :, :, lanes].reshape(rows, width) for slot in slots], axis=0)
        sides, tops = [], []
        for h in range(2):
            mine = low if h == 0 else jnp.logical_not(low)
            scores = lax.dot_general(
                jnp.where(mine, q, zero), keys, (((1,), (1,)), ((), ())), preferred_element_type=F32)
            most = jnp.max(scores, axis=-1, keepdims=True)
            probs = jnp.exp(scores - most).astype(BF16)
            sides.append(jnp.dot(probs, jnp.where(mine, keys, one), preferred_element_type=F32))
            tops.append(most)
        return (
            jnp.where(low, sides[0], sides[1]),
            pltpu.roll(jnp.where(low, sides[1], sides[0]), HEAD_DIM, 1),
            jnp.where(low, tops[0], tops[1]),
        )

    def merge(lanes, part):
        new_num, new_den, new_top = part
        old_top = top[:, lanes]
        both = jnp.maximum(old_top, new_top)
        keep, add = jnp.exp(old_top - both), jnp.exp(new_top - both)
        return num[:, lanes] * keep + new_num * add, den[:, lanes] * keep + new_den * add, both

    def attend(slots, start, stop):
        @pl.loop(start, stop)
        def _(pair):
            lanes = lanes_of(pair, width)
            part = read_part(lanes, slots)
            if 0 not in slots:
                part = merge(lanes, part)
            num[:, lanes], den[:, lanes], top[:, lanes] = part

    pairs = d // width
    for step in range(half - 1):
        slots = [0] if step == 0 else [step, n - step]
        split = pairs // 2 if step == half - 2 else 3 * pairs // 4
        attend(slots, 0, split)
        serve(step + 1)
        attend(slots, split, pairs)
        if step == half - 2:
            serve(half)
            for way in range(2):
                hand_copy(way, half, 1 - core).wait_recv()
        for way in range(2):
            hand_copy(way, step + 1, 1 - core).wait_recv()

    kinds = clusters.shape[0]
    every = states[...].reshape(n * rows, d + 128)
    grouped = lax.dot_general(every[:, d:], every[:, :d], (((0,), (0,)), ((), ())), preferred_element_type=F32)
    clusters[...] = rms_rows(grouped[:kinds]).astype(BF16)

    heads = 256 // kinds
    wide = heads * HEAD_DIM
    head_of = lax.broadcasted_iota(jnp.int32, (1, wide), 1) // HEAD_DIM

    @pl.loop(0, d // wide)
    def _(index):
        lanes = lanes_of(index, wide)
        q = tokens[:, lanes] * BF16(HEAD_DIM ** -0.5)
        mem = clusters[:, lanes]
        keys = jnp.concatenate([jnp.where(head_of == h, mem, zero) for h in range(heads)], axis=0)
        ones = jnp.concatenate(
            [jnp.broadcast_to(jnp.where(head_of == h, one, zero), (kinds, wide)) for h in range(heads)], axis=0)
        scores = lax.dot_general(q, keys, (((1,), (1,)), ((), ())), preferred_element_type=F32)
        column = lax.broadcasted_iota(jnp.int32, (1, heads * kinds), 1) // kinds
        shift = jnp.zeros_like(scores)
        for h in range(heads):
            most = jnp.max(jnp.where(column == h, scores, -jnp.inf), axis=-1, keepdims=True)
            shift = jnp.where(column == h, most, shift)
        probs = jnp.exp(scores - shift).astype(BF16)
        read = jnp.dot(probs, keys, preferred_element_type=F32) / jnp.dot(
            probs, ones, preferred_element_type=F32)
        for inner in range(wide // width):
            part_lanes = lanes_of(index * (wide // width) + inner, width)
            new_num, new_den, _ = merge(part_lanes, read_part(part_lanes, [half - 1, half + 1, half]))
            read_here = new_num / new_den + read[:, inner * width:(inner + 1) * width]
            readout[:, part_lanes] = read_here.astype(BF16)

    loads[2].wait()
    out_ref[...] = rms_rows(
        jnp.dot(readout[...], weights[...], preferred_element_type=F32)).astype(BF16)
    for copy in sends:
        copy.wait_send()


def on_device(tokens, span_bounds, mention_entity, entity_cluster, entity_table, w_out):
    n, groups = lax.axis_size("mem"), lax.axis_size("dp")
    rows, d = entity_table.shape
    count = mention_entity.shape[0]
    kinds = rows * n // CL_SIZE
    piece = d // PIECES
    vmem, anywhere = pl.BlockSpec(memory_space=pltpu.VMEM), pl.BlockSpec(memory_space=pl.ANY)
    dma = pltpu.SemaphoreType.DMA
    full = tokens.shape
    return pl.pallas_call(
        functools.partial(fused_kernel, n, groups),
        out_shape=jax.ShapeDtypeStruct(full, BF16),
        in_specs=[vmem] * 3 + [anywhere] * 3,
        out_specs=vmem,
        scratch_shapes=[
            pltpu.VMEM(full, BF16),
            pltpu.VMEM((rows, d), BF16),
            pltpu.VMEM(w_out.shape, BF16),
            pltpu.VMEM((n, SLOTS * PIECES, piece + 128), BF16),
            pltpu.VMEM((groups, n, SLOTS * PIECES, piece + 128), BF16),
            pltpu.VMEM((n, 4, rows // 4, d + 128), BF16),
            pltpu.VMEM((rows, d), F32),
            pltpu.VMEM((kinds, d), BF16),
            pltpu.VMEM(full, F32), pltpu.VMEM(full, F32), pltpu.VMEM(full, F32),
            pltpu.VMEM(full, BF16),
            dma((3,)),
            dma((n,)), dma((n,)), dma((groups,)), dma((groups,)), dma((groups,)), dma((groups,)), dma,
            dma((2, n)), dma((2, n)), dma((2, n)), dma((2, n)),
        ],
        compiler_params=pltpu.CompilerParams(
            collective_id=0, has_side_effects=True, vmem_limit_bytes=58 * 2**20),
    )(span_bounds, mention_entity.reshape(1, count), entity_cluster.reshape(1, rows), tokens, entity_table, w_out)


def solution(mesh):
    placed = (
        P(("dp", "mem"), None),
        P(None, ("dp", "mem")),
        P(("dp", "mem")),
        P("mem"),
        P("mem", None),
        P(),
    )
    return jax.shard_map(
        on_device, mesh=mesh, in_specs=placed, out_specs=P(("dp", "mem"), None), check_vma=False
    )
```

```python
import functools

import jax
import jax.numpy as jnp
from jax import lax
from jax.experimental import pallas as pl
from jax.experimental.pallas import tpu as pltpu
from jax.sharding import PartitionSpec as P

MESH = pl.DeviceIdType.MESH
HEAD_DIM = 64
CL_SIZE = 16
SLOTS = 4
PIECES = 4
BF16 = jnp.bfloat16
F32 = jnp.float32


def rms_rows(values):
    return values * lax.rsqrt(jnp.mean(values * values, axis=-1, keepdims=True) + 1e-06)


def ring_place(index, depth, width):
    z, y = index // width, index % width
    back = depth - 1 - z
    across = jnp.where(back % 2 == 0, y - 1, width - 1 - y)
    return jnp.where(y == 0, z, depth + back * (width - 1) + across)


def ring_device(place, depth, width):
    rest = jnp.maximum(place - depth, 0)
    back, across = rest // (width - 1), rest % (width - 1)
    y = jnp.where(back % 2 == 0, 1 + across, width - 1 - across)
    return jnp.where(place < depth, place * width, (depth - 1 - back) * width + y)


def fused_kernel(
    n, groups, bounds, ent_row, cluster_row, tokens_hbm, table_hbm, w_hbm,
    out_ref,
    tokens, table, weights, outbox, mentions, states, pooled, clusters, num, den, top, readout,
    load_sem, mem_send, mem_recv, dp_send, dp_recv, pair_send, pair_recv, own_sem,
    ring_send, ring_recv, hand_send, hand_recv,
):
    loads = [
        pltpu.make_async_copy(src, dst, load_sem.at[i])
        for i, (src, dst) in enumerate(((tokens_hbm, tokens), (table_hbm, table), (w_hbm, weights)))
    ]
    for load in loads:
        load.start()
    d = table.shape[1]
    rows = table.shape[0]
    piece = d // PIECES
    depth, width = 4, n // 4
    me, row = lax.axis_index("mem"), lax.axis_index("dp")
    core = row % 2
    sibling = row + 1 - 2 * core
    place = ring_place(me, depth, width)
    right = ring_device((place + 1) % n, depth, width)
    left = ring_device((place + n - 1) % n, depth, width)
    xs = groups // 2

    barrier = pltpu.get_barrier_semaphore()
    for step in range(1, n):
        pl.semaphore_signal(barrier, device_id=(row, (me + step) % n), device_id_type=MESH)
    for step in range(1, xs):
        pl.semaphore_signal(barrier, device_id=((row + 2 * step) % groups, me), device_id_type=MESH)
    pl.semaphore_signal(barrier, device_id=(sibling, me), device_id_type=MESH)

    count = bounds.shape[1]
    length = tokens.shape[0]
    total = n * SLOTS * PIECES
    position = lax.broadcasted_iota(jnp.int32, (length, count), 0)
    covered = ((position >= bounds[0:1, :]) & (position < bounds[1:2, :])).astype(F32).astype(BF16)
    spans = lax.dot_general(
        covered, jnp.ones((length, 128), BF16), (((0,), (0,)), ((), ())), preferred_element_type=F32)
    shard_row = ent_row[...] // rows
    owner = (lax.broadcasted_iota(jnp.int32, (n, count), 0) == shard_row).astype(F32)
    first = lax.broadcasted_iota(jnp.int32, (count, count), 0)
    second = lax.broadcasted_iota(jnp.int32, (count, count), 1)
    before = jnp.dot(
        owner.astype(BF16), (first < second).astype(F32).astype(BF16), preferred_element_type=F32)
    rank = jnp.sum(owner * before, axis=0, keepdims=True).astype(jnp.int32)
    slot_row = shard_row * SLOTS + rank
    loads[0].wait()
    sums = lax.dot_general(covered, tokens[...], (((0,), (0,)), ((), ())), preferred_element_type=F32)
    vectors = (sums / spans[:, 0:1]).astype(BF16)
    line = lax.broadcasted_iota(jnp.int32, (total, count), 0)
    match = slot_row == (line // (SLOTS * PIECES)) * SLOTS + line % SLOTS
    part = (line // SLOTS) % PIECES
    packed = jnp.zeros((total, piece), F32)
    for p in range(PIECES):
        pick = (match & (part == p)).astype(F32).astype(BF16)
        packed += jnp.dot(pick, vectors[:, p * piece:(p + 1) * piece], preferred_element_type=F32)
    local = (ent_row[...] - shard_row * rows + 1).astype(F32)
    ids = jnp.sum(jnp.where(match, local, 0.0), axis=1, keepdims=True) - 1.0
    outbox[:, :, :piece] = packed.astype(BF16).reshape(n, SLOTS * PIECES, piece)
    outbox[:, :, piece:] = jnp.broadcast_to(ids, (total, 128)).astype(BF16).reshape(n, SLOTS * PIECES, 128)

    pl.semaphore_wait(barrier, n - 1 + xs)

    own = pltpu.make_async_copy(outbox.at[me], mentions.at[row, me], own_sem)
    own.start()
    sends = []
    for step in range(1, n):
        to = (me + step) % n
        copy = pltpu.make_async_remote_copy(
            outbox.at[to], mentions.at[row, me], mem_send.at[step], mem_recv.at[step],
            device_id=(row, to), device_id_type=MESH)
        copy.start()
        sends.append(copy)
    own.wait()
    for step in range(1, n):
        src = (me + n - step) % n
        pltpu.make_async_remote_copy(
            outbox.at[src], mentions.at[row, src], mem_send.at[step], mem_recv.at[step],
            device_id=(row, src), device_id_type=MESH).wait_recv()

    def to_replica(block, to, send, recv):
        return pltpu.make_async_remote_copy(
            mentions.at[block], mentions.at[block], send, recv, device_id=(to, me), device_id_type=MESH)

    for step in range(1, xs):
        copy = to_replica(row, (row + 2 * step) % groups, dp_send.at[step], dp_recv.at[step])
        copy.start()
        sends.append(copy)
    copy = to_replica(row, sibling, pair_send.at[0], pair_recv.at[0])
    copy.start()
    sends.append(copy)
    for step in range(1, xs):
        src = (row + groups - 2 * step) % groups
        to_replica(src, src, dp_send.at[step], dp_recv.at[step]).wait_recv()
        copy = to_replica(src, sibling, pair_send.at[step], pair_recv.at[step])
        copy.start()
        sends.append(copy)
    for step in range(xs):
        src = (sibling + groups - 2 * step) % groups
        to_replica(src, sibling, pair_send.at[step], pair_recv.at[step]).wait_recv()

    loads[1].wait()
    arrived = groups * n * SLOTS * PIECES
    box = mentions[...].reshape(arrived, piece + 128)
    line = lax.broadcasted_iota(jnp.int32, (arrived, rows), 0)
    entity = lax.broadcasted_iota(jnp.int32, (arrived, rows), 1).astype(F32)
    named = box[:, piece:].astype(F32) == entity
    part = (line // SLOTS) % PIECES
    square = jnp.zeros((rows, 1), F32)
    for p in range(PIECES):
        pick = (named & (part == p)).astype(F32).astype(BF16)
        got = lax.dot_general(pick, box[:, :piece], (((0,), (0,)), ((), ())), preferred_element_type=F32)
        got += table[:, p * piece:(p + 1) * piece].astype(F32)
        pooled[:, p * piece:(p + 1) * piece] = got
        square += jnp.sum(got * got, axis=-1, keepdims=True)
    state = (pooled[...] * lax.rsqrt(square / d + 1e-06)).astype(BF16)
    quarter = rows // 4
    states[0, :, :, :d] = state.reshape(4, quarter, d)
    kind = lax.broadcasted_iota(jnp.int32, (128, rows), 0)
    group = (cluster_row[...] == kind).astype(F32).T.astype(BF16)
    states[0, :, :, d:] = group.reshape(4, quarter, 128)

    half = n // 2

    def portion(way, step):
        if step < half:
            return pl.ds(2 * core, 2)
        return pl.ds(2 * core + way, 1)

    def ring_copy(way, step):
        src = step - 1 if way == 0 else (n - step + 1) % n
        dst = step if way == 0 else n - step
        quarters = portion(way, step)
        return pltpu.make_async_remote_copy(
            states.at[src, quarters], states.at[dst, quarters], ring_send.at[way, step], ring_recv.at[way, step],
            device_id=(row, right if way == 0 else left), device_id_type=MESH)

    def hand_copy(way, step, to_core):
        dst = step if way == 0 else n - step
        if step < half:
            quarters = pl.ds(2 * to_core, 2)
        else:
            quarters = pl.ds(2 * to_core + way, 1)
        return pltpu.make_async_remote_copy(
            states.at[dst, quarters], states.at[dst, quarters], hand_send.at[way, step], hand_recv.at[way, step],
            device_id=(sibling, me), device_id_type=MESH)

    def serve(step):
        for way in range(2):
            ring_copy(way, step).wait_recv()
            if step < half:
                copy = ring_copy(way, step + 1)
                copy.start()
                sends.append(copy)
            copy = hand_copy(way, step, core)
            copy.start()
            sends.append(copy)

    for way in range(2):
        copy = ring_copy(way, 1)
        copy.start()
        sends.append(copy)

    width = 2 * HEAD_DIM
    low = lax.broadcasted_iota(jnp.int32, (1, width), 1) < HEAD_DIM
    one, zero = jnp.ones((), BF16), jnp.zeros((), BF16)

    def lanes_of(index, size):
        return pl.ds(pl.multiple_of(index * size, size), size)

    def read_part(lanes, slots):
        q = tokens[:, lanes] * BF16(HEAD_DIM ** -0.5)
        keys = jnp.concatenate([states[slot, :, :, lanes].reshape(rows, width) for slot in slots], axis=0)
        sides, tops = [], []
        for h in range(2):
            mine = low if h == 0 else jnp.logical_not(low)
            scores = lax.dot_general(
                jnp.where(mine, q, zero), keys, (((1,), (1,)), ((), ())), preferred_element_type=F32)
            most = jnp.max(scores, axis=-1, keepdims=True)
            probs = jnp.exp(scores - most).astype(BF16)
            sides.append(jnp.dot(probs, jnp.where(mine, keys, one), preferred_element_type=F32))
            tops.append(most)
        return (
            jnp.where(low, sides[0], sides[1]),
            pltpu.roll(jnp.where(low, sides[1], sides[0]), HEAD_DIM, 1),
            jnp.where(low, tops[0], tops[1]),
        )

    def merge(lanes, part):
        new_num, new_den, new_top = part
        old_top = top[:, lanes]
        both = jnp.maximum(old_top, new_top)
        keep, add = jnp.exp(old_top - both), jnp.exp(new_top - both)
        return num[:, lanes] * keep + new_num * add, den[:, lanes] * keep + new_den * add, both

    def attend(slots, start, stop):
        @pl.loop(start, stop, unroll=4 if slots == [0] else 2)
        def _(pair):
            lanes = lanes_of(pair, width)
            part = read_part(lanes, slots)
            if 0 not in slots:
                part = merge(lanes, part)
            num[:, lanes], den[:, lanes], top[:, lanes] = part

    pairs = d // width
    attend([0], 0, 3 * pairs // 4)
    serve(1)
    attend([0], 3 * pairs // 4, pairs)
    early = []
    for step in range(1, half - 1):
        if step > 1:
            serve(step)
        early += [step, n - step]
    for step in range(1, half - 1):
        for way in range(2):
            hand_copy(way, step, 1 - core).wait_recv()
    attend(early, 0, pairs // 2)
    serve(half - 1)
    attend(early, pairs // 2, 7 * pairs // 8)
    serve(half)
    attend(early, 7 * pairs // 8, pairs)
    for step in range(half - 1, half + 1):
        for way in range(2):
            hand_copy(way, step, 1 - core).wait_recv()

    kinds = clusters.shape[0]
    every = states[...].reshape(n * rows, d + 128)
    grouped = lax.dot_general(every[:, d:], every[:, :d], (((0,), (0,)), ((), ())), preferred_element_type=F32)
    clusters[...] = rms_rows(grouped[:kinds]).astype(BF16)

    heads = 256 // kinds
    wide = heads * HEAD_DIM
    head_of = lax.broadcasted_iota(jnp.int32, (1, wide), 1) // HEAD_DIM

    @pl.loop(0, d // wide)
    def _(index):
        lanes = lanes_of(index, wide)
        q = tokens[:, lanes] * BF16(HEAD_DIM ** -0.5)
        mem = clusters[:, lanes]
        keys = jnp.concatenate([jnp.where(head_of == h, mem, zero) for h in range(heads)], axis=0)
        ones = jnp.concatenate(
            [jnp.broadcast_to(jnp.where(head_of == h, one, zero), (kinds, wide)) for h in range(heads)], axis=0)
        scores = lax.dot_general(q, keys, (((1,), (1,)), ((), ())), preferred_element_type=F32)
        column = lax.broadcasted_iota(jnp.int32, (1, heads * kinds), 1) // kinds
        shift = jnp.zeros_like(scores)
        for h in range(heads):
            most = jnp.max(jnp.where(column == h, scores, -jnp.inf), axis=-1, keepdims=True)
            shift = jnp.where(column == h, most, shift)
        probs = jnp.exp(scores - shift).astype(BF16)
        read = jnp.dot(probs, keys, preferred_element_type=F32) / jnp.dot(
            probs, ones, preferred_element_type=F32)
        for inner in range(wide // width):
            part_lanes = lanes_of(index * (wide // width) + inner, width)
            new_num, new_den, _ = merge(part_lanes, read_part(part_lanes, [half - 1, half + 1, half]))
            read_here = new_num / new_den + read[:, inner * width:(inner + 1) * width]
            readout[:, part_lanes] = read_here.astype(BF16)

    loads[2].wait()
    out_ref[...] = rms_rows(
        jnp.dot(readout[...], weights[...], preferred_element_type=F32)).astype(BF16)
    for copy in sends:
        copy.wait_send()


def on_device(tokens, span_bounds, mention_entity, entity_cluster, entity_table, w_out):
    n, groups = lax.axis_size("mem"), lax.axis_size("dp")
    rows, d = entity_table.shape
    count = mention_entity.shape[0]
    kinds = rows * n // CL_SIZE
    piece = d // PIECES
    vmem, anywhere = pl.BlockSpec(memory_space=pltpu.VMEM), pl.BlockSpec(memory_space=pl.ANY)
    dma = pltpu.SemaphoreType.DMA
    full = tokens.shape
    return pl.pallas_call(
        functools.partial(fused_kernel, n, groups),
        out_shape=jax.ShapeDtypeStruct(full, BF16),
        in_specs=[vmem] * 3 + [anywhere] * 3,
        out_specs=vmem,
        scratch_shapes=[
            pltpu.VMEM(full, BF16),
            pltpu.VMEM((rows, d), BF16),
            pltpu.VMEM(w_out.shape, BF16),
            pltpu.VMEM((n, SLOTS * PIECES, piece + 128), BF16),
            pltpu.VMEM((groups, n, SLOTS * PIECES, piece + 128), BF16),
            pltpu.VMEM((n, 4, rows // 4, d + 128), BF16),
            pltpu.VMEM((rows, d), F32),
            pltpu.VMEM((kinds, d), BF16),
            pltpu.VMEM(full, F32), pltpu.VMEM(full, F32), pltpu.VMEM(full, F32),
            pltpu.VMEM(full, BF16),
            dma((3,)),
            dma((n,)), dma((n,)), dma((groups,)), dma((groups,)), dma((groups,)), dma((groups,)), dma,
            dma((2, n)), dma((2, n)), dma((2, n)), dma((2, n)),
        ],
        compiler_params=pltpu.CompilerParams(
            collective_id=0, has_side_effects=True, vmem_limit_bytes=58 * 2**20),
    )(span_bounds, mention_entity.reshape(1, count), entity_cluster.reshape(1, rows), tokens, entity_table, w_out)


def solution(mesh):
    placed = (
        P(("dp", "mem"), None),
        P(None, ("dp", "mem")),
        P(("dp", "mem")),
        P("mem"),
        P("mem", None),
        P(),
    )
    return jax.shard_map(
        on_device, mesh=mesh, in_specs=placed, out_specs=P(("dp", "mem"), None), check_vma=False
    )
```

```python
import functools

import jax
import jax.numpy as jnp
from jax import lax
from jax.experimental import pallas as pl
from jax.experimental.pallas import tpu as pltpu
from jax.sharding import PartitionSpec as P

MESH = pl.DeviceIdType.MESH
HEAD_DIM = 64
CL_SIZE = 16
SLOTS = 4
PIECES = 4
BF16 = jnp.bfloat16
F32 = jnp.float32


def rms_rows(values):
    return values * lax.rsqrt(jnp.mean(values * values, axis=-1, keepdims=True) + 1e-06)


def ring_place(index, depth, width):
    z, y = index // width, index % width
    back = depth - 1 - z
    across = jnp.where(back % 2 == 0, y - 1, width - 1 - y)
    return jnp.where(y == 0, z, depth + back * (width - 1) + across)


def ring_device(place, depth, width):
    rest = jnp.maximum(place - depth, 0)
    back, across = rest // (width - 1), rest % (width - 1)
    y = jnp.where(back % 2 == 0, 1 + across, width - 1 - across)
    return jnp.where(place < depth, place * width, (depth - 1 - back) * width + y)


def fused_kernel(
    n, groups, bounds, ent_row, cluster_row, tokens_hbm, table_hbm, w_hbm,
    out_ref,
    tokens, table, weights, outbox, mentions, states, pooled, clusters, num, den, top, readout,
    load_sem, mem_send, mem_recv, dp_send, dp_recv, pair_send, pair_recv, own_sem,
    ring_send, ring_recv, hand_send, hand_recv,
):
    loads = [
        pltpu.make_async_copy(src, dst, load_sem.at[i])
        for i, (src, dst) in enumerate(((tokens_hbm, tokens), (table_hbm, table), (w_hbm, weights)))
    ]
    for load in loads:
        load.start()
    d = table.shape[1]
    rows = table.shape[0]
    piece = d // PIECES
    depth, width = 4, n // 4
    me, row = lax.axis_index("mem"), lax.axis_index("dp")
    core = row % 2
    sibling = row + 1 - 2 * core
    place = ring_place(me, depth, width)
    right = ring_device((place + 1) % n, depth, width)
    left = ring_device((place + n - 1) % n, depth, width)
    xs = groups // 2

    barrier = pltpu.get_barrier_semaphore()
    for step in range(1, n):
        pl.semaphore_signal(barrier, device_id=(row, (me + step) % n), device_id_type=MESH)
    for step in range(1, xs):
        pl.semaphore_signal(barrier, device_id=((row + 2 * step) % groups, me), device_id_type=MESH)
    pl.semaphore_signal(barrier, device_id=(sibling, me), device_id_type=MESH)

    count = bounds.shape[1]
    length = tokens.shape[0]
    total = n * SLOTS * PIECES
    position = lax.broadcasted_iota(jnp.int32, (length, count), 0)
    covered = ((position >= bounds[0:1, :]) & (position < bounds[1:2, :])).astype(F32).astype(BF16)
    spans = lax.dot_general(
        covered, jnp.ones((length, 128), BF16), (((0,), (0,)), ((), ())), preferred_element_type=F32)
    shard_row = ent_row[...] // rows
    owner = (lax.broadcasted_iota(jnp.int32, (n, count), 0) == shard_row).astype(F32)
    first = lax.broadcasted_iota(jnp.int32, (count, count), 0)
    second = lax.broadcasted_iota(jnp.int32, (count, count), 1)
    before = jnp.dot(
        owner.astype(BF16), (first < second).astype(F32).astype(BF16), preferred_element_type=F32)
    rank = jnp.sum(owner * before, axis=0, keepdims=True).astype(jnp.int32)
    slot_row = shard_row * SLOTS + rank
    loads[0].wait()
    sums = lax.dot_general(covered, tokens[...], (((0,), (0,)), ((), ())), preferred_element_type=F32)
    vectors = (sums / spans[:, 0:1]).astype(BF16)
    line = lax.broadcasted_iota(jnp.int32, (total, count), 0)
    match = slot_row == (line // (SLOTS * PIECES)) * SLOTS + line % SLOTS
    part = (line // SLOTS) % PIECES
    packed = jnp.zeros((total, piece), F32)
    for p in range(PIECES):
        pick = (match & (part == p)).astype(F32).astype(BF16)
        packed += jnp.dot(pick, vectors[:, p * piece:(p + 1) * piece], preferred_element_type=F32)
    local = (ent_row[...] - shard_row * rows + 1).astype(F32)
    ids = jnp.sum(jnp.where(match, local, 0.0), axis=1, keepdims=True) - 1.0
    outbox[:, :, :piece] = packed.astype(BF16).reshape(n, SLOTS * PIECES, piece)
    outbox[:, :, piece:] = jnp.broadcast_to(ids, (total, 128)).astype(BF16).reshape(n, SLOTS * PIECES, 128)

    pl.semaphore_wait(barrier, n - 1 + xs)

    own = pltpu.make_async_copy(outbox.at[me], mentions.at[row, me], own_sem)
    own.start()
    sends = []
    for step in range(1, n):
        to = (me + step) % n
        copy = pltpu.make_async_remote_copy(
            outbox.at[to], mentions.at[row, me], mem_send.at[step], mem_recv.at[step],
            device_id=(row, to), device_id_type=MESH)
        copy.start()
        sends.append(copy)
    own.wait()
    for step in range(1, n):
        src = (me + n - step) % n
        pltpu.make_async_remote_copy(
            outbox.at[src], mentions.at[row, src], mem_send.at[step], mem_recv.at[step],
            device_id=(row, src), device_id_type=MESH).wait_recv()

    def to_replica(block, to, send, recv):
        return pltpu.make_async_remote_copy(
            mentions.at[block], mentions.at[block], send, recv, device_id=(to, me), device_id_type=MESH)

    for step in range(1, xs):
        copy = to_replica(row, (row + 2 * step) % groups, dp_send.at[step], dp_recv.at[step])
        copy.start()
        sends.append(copy)
    copy = to_replica(row, sibling, pair_send.at[0], pair_recv.at[0])
    copy.start()
    sends.append(copy)
    for step in range(1, xs):
        src = (row + groups - 2 * step) % groups
        to_replica(src, src, dp_send.at[step], dp_recv.at[step]).wait_recv()
        copy = to_replica(src, sibling, pair_send.at[step], pair_recv.at[step])
        copy.start()
        sends.append(copy)
    for step in range(xs):
        src = (sibling + groups - 2 * step) % groups
        to_replica(src, sibling, pair_send.at[step], pair_recv.at[step]).wait_recv()

    loads[1].wait()
    arrived = groups * n * SLOTS * PIECES
    box = mentions[...].reshape(arrived, piece + 128)
    line = lax.broadcasted_iota(jnp.int32, (arrived, rows), 0)
    entity = lax.broadcasted_iota(jnp.int32, (arrived, rows), 1).astype(F32)
    named = box[:, piece:].astype(F32) == entity
    part = (line // SLOTS) % PIECES
    square = jnp.zeros((rows, 1), F32)
    for p in range(PIECES):
        pick = (named & (part == p)).astype(F32).astype(BF16)
        got = lax.dot_general(pick, box[:, :piece], (((0,), (0,)), ((), ())), preferred_element_type=F32)
        got += table[:, p * piece:(p + 1) * piece].astype(F32)
        pooled[:, p * piece:(p + 1) * piece] = got
        square += jnp.sum(got * got, axis=-1, keepdims=True)
    state = (pooled[...] * lax.rsqrt(square / d + 1e-06)).astype(BF16)
    quarter = rows // 4
    states[0, :, :, :d] = state.reshape(4, quarter, d)
    kind = lax.broadcasted_iota(jnp.int32, (128, rows), 0)
    group = (cluster_row[...] == kind).astype(F32).T.astype(BF16)
    states[0, :, :, d:] = group.reshape(4, quarter, 128)

    half = n // 2

    def portion(way, step):
        if step < half:
            return pl.ds(2 * core, 2)
        return pl.ds(2 * core + way, 1)

    def ring_copy(way, step):
        src = step - 1 if way == 0 else (n - step + 1) % n
        dst = step if way == 0 else n - step
        quarters = portion(way, step)
        return pltpu.make_async_remote_copy(
            states.at[src, quarters], states.at[dst, quarters], ring_send.at[way, step], ring_recv.at[way, step],
            device_id=(row, right if way == 0 else left), device_id_type=MESH)

    def hand_copy(way, step, to_core):
        dst = step if way == 0 else n - step
        if step < half:
            quarters = pl.ds(2 * to_core, 2)
        else:
            quarters = pl.ds(2 * to_core + way, 1)
        return pltpu.make_async_remote_copy(
            states.at[dst, quarters], states.at[dst, quarters], hand_send.at[way, step], hand_recv.at[way, step],
            device_id=(sibling, me), device_id_type=MESH)

    def serve(step):
        for way in range(2):
            ring_copy(way, step).wait_recv()
            if step < half:
                ring_copy(way, step + 1).start()
            hand_copy(way, step, core).start()

    for way in range(2):
        ring_copy(way, 1).start()

    width = 2 * HEAD_DIM
    low = lax.broadcasted_iota(jnp.int32, (1, width), 1) < HEAD_DIM
    one, zero = jnp.ones((), BF16), jnp.zeros((), BF16)

    def lanes_of(index, size):
        return pl.ds(pl.multiple_of(index * size, size), size)

    def read_part(lanes, slots):
        q = tokens[:, lanes] * BF16(HEAD_DIM ** -0.5)
        keys = jnp.concatenate([states[slot, :, :, lanes].reshape(rows, width) for slot in slots], axis=0)
        sides, tops = [], []
        for h in range(2):
            mine = low if h == 0 else jnp.logical_not(low)
            scores = lax.dot_general(
                jnp.where(mine, q, zero), keys, (((1,), (1,)), ((), ())), preferred_element_type=F32)
            most = jnp.max(scores, axis=-1, keepdims=True)
            probs = jnp.exp(scores - most).astype(BF16)
            sides.append(jnp.dot(probs, jnp.where(mine, keys, one), preferred_element_type=F32))
            tops.append(most)
        return (
            jnp.where(low, sides[0], sides[1]),
            pltpu.roll(jnp.where(low, sides[1], sides[0]), HEAD_DIM, 1),
            jnp.where(low, tops[0], tops[1]),
        )

    def merge(lanes, part):
        new_num, new_den, new_top = part
        old_top = top[:, lanes]
        both = jnp.maximum(old_top, new_top)
        keep, add = jnp.exp(old_top - both), jnp.exp(new_top - both)
        return num[:, lanes] * keep + new_num * add, den[:, lanes] * keep + new_den * add, both

    def attend(slots, group, served):
        @pl.loop(0, d // width // group)
        def _(index):
            for inner in range(group):
                lanes = lanes_of(index * group + inner, width)
                part = read_part(lanes, slots)
                if 0 not in slots:
                    part = merge(lanes, part)
                num[:, lanes], den[:, lanes], top[:, lanes] = part
            for last, step in served:
                @pl.when(index == last)
                def _():
                    serve(step)

    pairs = d // width
    attend([0], 4, [(pairs // 4 - 2, 1)])
    early = []
    for step in range(1, half - 1):
        if step > 1:
            serve(step)
        early += [step, n - step]
    for step in range(1, half - 1):
        for way in range(2):
            hand_copy(way, step, 1 - core).wait_recv()
    attend(early, 2, [(pairs // 4 - 1, half - 1), (pairs // 2 - 2, half)])
    for step in range(half - 1, half + 1):
        for way in range(2):
            hand_copy(way, step, 1 - core).wait_recv()

    kinds = clusters.shape[0]
    every = states[...].reshape(n * rows, d + 128)
    grouped = lax.dot_general(every[:, d:], every[:, :d], (((0,), (0,)), ((), ())), preferred_element_type=F32)
    clusters[...] = rms_rows(grouped[:kinds]).astype(BF16)

    heads = 256 // kinds
    wide = heads * HEAD_DIM
    head_of = lax.broadcasted_iota(jnp.int32, (1, wide), 1) // HEAD_DIM

    @pl.loop(0, d // wide)
    def _(index):
        lanes = lanes_of(index, wide)
        q = tokens[:, lanes] * BF16(HEAD_DIM ** -0.5)
        mem = clusters[:, lanes]
        keys = jnp.concatenate([jnp.where(head_of == h, mem, zero) for h in range(heads)], axis=0)
        ones = jnp.concatenate(
            [jnp.broadcast_to(jnp.where(head_of == h, one, zero), (kinds, wide)) for h in range(heads)], axis=0)
        scores = lax.dot_general(q, keys, (((1,), (1,)), ((), ())), preferred_element_type=F32)
        column = lax.broadcasted_iota(jnp.int32, (1, heads * kinds), 1) // kinds
        shift = jnp.zeros_like(scores)
        for h in range(heads):
            most = jnp.max(jnp.where(column == h, scores, -jnp.inf), axis=-1, keepdims=True)
            shift = jnp.where(column == h, most, shift)
        probs = jnp.exp(scores - shift).astype(BF16)
        read = jnp.dot(probs, keys, preferred_element_type=F32) / jnp.dot(
            probs, ones, preferred_element_type=F32)
        for inner in range(wide // width):
            part_lanes = lanes_of(index * (wide // width) + inner, width)
            new_num, new_den, _ = merge(part_lanes, read_part(part_lanes, [half - 1, half + 1, half]))
            read_here = new_num / new_den + read[:, inner * width:(inner + 1) * width]
            readout[:, part_lanes] = read_here.astype(BF16)

    loads[2].wait()
    out_ref[...] = rms_rows(
        jnp.dot(readout[...], weights[...], preferred_element_type=F32)).astype(BF16)
    for copy in sends:
        copy.wait_send()
    for step in range(1, half + 1):
        for way in range(2):
            ring_copy(way, step).wait_send()
            hand_copy(way, step, core).wait_send()


def on_device(tokens, span_bounds, mention_entity, entity_cluster, entity_table, w_out):
    n, groups = lax.axis_size("mem"), lax.axis_size("dp")
    rows, d = entity_table.shape
    count = mention_entity.shape[0]
    kinds = rows * n // CL_SIZE
    piece = d // PIECES
    vmem, anywhere = pl.BlockSpec(memory_space=pltpu.VMEM), pl.BlockSpec(memory_space=pl.ANY)
    dma = pltpu.SemaphoreType.DMA
    full = tokens.shape
    return pl.pallas_call(
        functools.partial(fused_kernel, n, groups),
        out_shape=jax.ShapeDtypeStruct(full, BF16),
        in_specs=[vmem] * 3 + [anywhere] * 3,
        out_specs=vmem,
        scratch_shapes=[
            pltpu.VMEM(full, BF16),
            pltpu.VMEM((rows, d), BF16),
            pltpu.VMEM(w_out.shape, BF16),
            pltpu.VMEM((n, SLOTS * PIECES, piece + 128), BF16),
            pltpu.VMEM((groups, n, SLOTS * PIECES, piece + 128), BF16),
            pltpu.VMEM((n, 4, rows // 4, d + 128), BF16),
            pltpu.VMEM((rows, d), F32),
            pltpu.VMEM((kinds, d), BF16),
            pltpu.VMEM(full, F32), pltpu.VMEM(full, F32), pltpu.VMEM(full, F32),
            pltpu.VMEM(full, BF16),
            dma((3,)),
            dma((n,)), dma((n,)), dma((groups,)), dma((groups,)), dma((groups,)), dma((groups,)), dma,
            dma((2, n)), dma((2, n)), dma((2, n)), dma((2, n)),
        ],
        compiler_params=pltpu.CompilerParams(
            collective_id=0, has_side_effects=True, vmem_limit_bytes=58 * 2**20),
    )(span_bounds, mention_entity.reshape(1, count), entity_cluster.reshape(1, rows), tokens, entity_table, w_out)


def solution(mesh):
    placed = (
        P(("dp", "mem"), None),
        P(None, ("dp", "mem")),
        P(("dp", "mem")),
        P("mem"),
        P("mem", None),
        P(),
    )
    return jax.shard_map(
        on_device, mesh=mesh, in_specs=placed, out_specs=P(("dp", "mem"), None), check_vma=False
    )
```
